256 devices in a mesh: snode: 64 (over z, x, core), panel: 4 (over y).
Axes of the slice: x: 4, y: 4, z: 8, core: 2. Of those that a mesh axis runs over, the one named last changes fastest.
Arguments:
- top_inverse: float32 [1280, 1280], P('panel')
- diag_inverse: float32 [3, 64, 512, 512], P(None, 'snode', 'panel')
- u_factor: float32 [3, 64, 768, 512], P(None, 'snode'), may hold values from -0.21875 to 0.21875
- parent_map: int32 [2, 64], replicated, may hold values from 0 to 63, as said below
- lengths: int32 [3, 64], replicated, may hold values from 192 to 768, as said below
- rows_map: int32 [3, 64, 768], replicated, may hold values from 0 to 1279, as said below
Outputs:
- diag_block: float32 [3, 64, 512, 512], P(None, 'snode', 'panel')
- off_block: float32 [3, 64, 768, 512], P(None, 'snode', 'panel')
The draws below stay inside these ranges and needn't reach their ends.
Inputs may be any that keep to these rules, and one draw needn't show every extreme that they name: `parent_map`: supernode n of a level is held on snode device n. The parent of a supernode of level l + 1 is held on the same device or on the one before it along snode, the last device standing before the first. `lengths`: every level has a supernode with exactly 768 live structure rows. `top_inverse` and every `diag_inverse[l, n]` are symmetric (each is the inverse of a symmetric positive definite matrix), so every full_block is symmetric. For a below lengths[l, n], the entries rows_map[l, n, a] are distinct and lie below 512 plus the parent's length (1280 at level 0); entries from the length on are 0.
All inputs are finite; a program needn't handle non-finite values.
Results may differ from the reference program's by a relative error of at most 0.0003.
Values sent between devices are 32-bit elements; how exact they have to be, the bound alone decides.
A program may use at most 128 MiB of HBM per device.

```python
import jax
import jax.numpy as jnp
from jax import lax

B = 512
SR = 768
LEV = 3
SLOT = 1
NODES_L = 64


def structure(key):
    key_len, key_back, key_slot, key_pick, key_long = jax.random.split(key, 5)
    live_count = jax.random.randint(key_len, (LEV, NODES_L), SR // 4, SR + 1)
    longest = jax.random.randint(key_long, (LEV, 1), 0, NODES_L)
    node_iota = jnp.arange(NODES_L, dtype=jnp.int32)[None, :]
    live_count = jnp.where(node_iota == longest, SR, live_count).astype(jnp.int32)
    owner_count = NODES_L // SLOT
    node_owner = jnp.arange(NODES_L, dtype=jnp.int32) // SLOT
    step_back = jax.random.randint(key_back, (LEV - 1, NODES_L), 0, 2)
    parent_slot = jax.random.randint(key_slot, (LEV - 1, NODES_L), 0, SLOT)
    parent_owner = (node_owner[None, :] - step_back) % owner_count
    parents = (parent_owner * SLOT + parent_slot).astype(jnp.int32)
    upper_len = jnp.take_along_axis(live_count[:-1], parents, axis=1)
    parent_len = jnp.concatenate([jnp.full((1, NODES_L), SR, jnp.int32), upper_len], axis=0)
    row_total = B + SR
    total_iota = jnp.arange(row_total, dtype=jnp.int32)
    scores = jax.random.randint(key_pick, (LEV, NODES_L, row_total), 0, 1 << 19) * row_total + total_iota
    scores = jnp.where(total_iota >= (B + parent_len)[..., None], scores + (1 << 30), scores)
    ordered = jnp.argsort(scores, axis=-1)[..., :SR].astype(jnp.int32)
    live_mask = jnp.arange(SR, dtype=jnp.int32)[None, None, :] < live_count[..., None]
    row_lists = jnp.where(live_mask, ordered, 0).astype(jnp.int32)
    return (live_count, parents, row_lists)


def draw_parent_map(key, part):
    live_count, parents, row_lists = structure(key)
    return parents


def draw_lengths(key, part):
    live_count, parents, row_lists = structure(key)
    return live_count


def draw_rows_map(key, part):
    live_count, parents, row_lists = structure(key)
    return row_lists


def dense_block(key, lead_shape, order, diag_low, diag_high):
    key_off, key_diag = jax.random.split(key, 2)
    raw = jax.random.uniform(key_off, lead_shape + (order, order), jnp.float32, -1.0, 1.0)
    sym = (raw + jnp.swapaxes(raw, -1, -2)) * (0.5 * (6.0 / order) ** 0.5)
    diagonal = jax.random.uniform(key_diag, lead_shape + (order,), jnp.float32, diag_low, diag_high)
    identity = jnp.eye(order, dtype=jnp.float32)
    return sym * (1.0 - identity) + diagonal[..., :, None] * identity


def draw_top_inverse(key, part):
    key = jax.random.fold_in(key, 11)
    return dense_block(key, (), B + SR, 2.6, 3.6)


def draw_diag_inverse(key, part):
    key = jax.random.fold_in(key, 23)
    return dense_block(key, (LEV, NODES_L), B, 2.6, 3.6)


def block_levels(stream_key, dims, pieces, smallest, largest):
    gain = 1.0
    for position, shards_of in pieces:
        heights = jax.random.uniform(jax.random.fold_in(jax.random.fold_in(stream_key, 6), position), (shards_of,), jnp.float32, smallest / len(pieces), largest / len(pieces))
        gain = gain * jnp.repeat(jnp.exp(heights), dims[position] // shards_of).reshape((-1,) + (1,) * (len(dims) - 1 - position))
    return gain


def bell_draw(stream_key, shape, spread, reach, pieces=(), held_as=jnp.bfloat16):
    gain = block_levels(stream_key, shape, pieces, -0.22, 0.18) if pieces else 1.0
    entries = jax.random.normal(stream_key, shape, jnp.float32) * spread * gain
    return jnp.minimum(jnp.maximum(entries, -reach), reach).astype(held_as)


def setup_inputs(seed: int = 0) -> dict:
    key_list = jax.random.split(jax.random.key(seed), 7)
    top_inverse = draw_top_inverse(jax.random.fold_in(key_list[6], 71), 0)
    diag_inverse = draw_diag_inverse(jax.random.fold_in(key_list[6], 71), 0)
    u_factor = bell_draw(key_list[2], (LEV, NODES_L, SR, B), SR ** -0.5, 0.21875, ((1, 64),), jnp.float32)
    parent_map = draw_parent_map(jax.random.fold_in(key_list[6], 71), 0)
    lengths = draw_lengths(jax.random.fold_in(key_list[6], 71), 0)
    rows_map = draw_rows_map(jax.random.fold_in(key_list[6], 71), 0)
    return dict(top_inverse=top_inverse, diag_inverse=diag_inverse, u_factor=u_factor, parent_map=parent_map, lengths=lengths, rows_map=rows_map)


HIGHEST = lax.Precision.HIGHEST


def extract_block(parent_block, row_index, live_rows):
    row_total = row_index.shape[0]
    live_mask = (jnp.arange(row_total, dtype=jnp.int32) < live_rows).astype(parent_block.dtype)
    picked = jnp.take(jnp.take(parent_block, row_index, axis=0), row_index, axis=1)
    return picked * live_mask[:, None] * live_mask[None, :]


def assemble(diag_part, off_part, inner_part):
    upper_rows = jnp.concatenate([diag_part, off_part.T], axis=1)
    lower_rows = jnp.concatenate([off_part, inner_part], axis=1)
    return jnp.concatenate([upper_rows, lower_rows], axis=0)


def reference(top_inverse, diag_inverse, u_factor, parent_map, lengths, rows_map):
    diag_tiers = []
    off_tiers = []
    blocks_prev = None
    for tier_index in range(LEV):
        def solve_one(node_index, tier_index=tier_index, blocks_prev=blocks_prev):
            if tier_index == 0:
                parent_block = top_inverse
            else:
                parent_block = blocks_prev[parent_map[tier_index - 1, node_index]]
            inner_block = extract_block(parent_block, rows_map[tier_index, node_index], lengths[tier_index, node_index])
            u_block = u_factor[tier_index, node_index]
            off_part = -jnp.dot(inner_block, u_block, precision=HIGHEST)
            diag_part = diag_inverse[tier_index, node_index] - jnp.dot(u_block.T, off_part, precision=HIGHEST)
            return diag_part, off_part, assemble(diag_part, off_part, inner_block)
        diag_stack, off_stack, blocks_prev = lax.map(solve_one, jnp.arange(NODES_L, dtype=jnp.int32))
        diag_tiers.append(diag_stack)
        off_tiers.append(off_stack)
    return jnp.stack(diag_tiers), jnp.stack(off_tiers)
```

```python
import functools

import jax
import jax.numpy as jnp
from jax import lax
from jax.experimental import pallas as pl
from jax.experimental.pallas import tpu as pltpu
from jax.sharding import PartitionSpec as P

F32 = jnp.float32
BF16 = jnp.bfloat16
MESH = pl.DeviceIdType.MESH

T = 1280
B = 512
SR = 768
J0 = T
J1 = T + B
N2 = T + 2 * B
SHARD = T // 4
HALF = SHARD // 2
SUB = HALF // 2
RQ = SR // 4
BQ = B // 4


def split(x):
    hi = x.astype(BF16)
    return hi, (x - hi.astype(F32)).astype(BF16)


def mm(a, b):
    return jnp.dot(a, b, preferred_element_type=F32)


def mm3(a, bh, bl):
    ah, al = split(a)
    return mm(ah, bh) + (mm(ah, bl) + mm(al, bh))


def mmf(a, b):
    bh, bl = split(b)
    return mm3(a, bh, bl)


def one_hot(g, base, rows):
    at = lax.broadcasted_iota(jnp.int32, (rows, SR), 0) + base
    return jnp.where(at == g, 1.0, 0.0).astype(BF16)


def compose(h, pos):
    column = jnp.broadcast_to(h.astype(F32), (128, SR)).T
    at = lax.broadcasted_iota(jnp.int32, (SR, 128), 0)
    parts = []
    for block in range(SR // 128):
        hit = at == pos[:, 128 * block:128 * (block + 1)]
        parts.append(jnp.sum(jnp.where(hit, column, 0.0), axis=0, keepdims=True))
    return jnp.concatenate(parts, axis=1).astype(jnp.int32)


def kernel(
    top, dinv, ufac, pm, ln, rm,
    diag_out, off_out,
    z, u0, u0r, u1, u2, uh, ul, v0h, v0l, v1h, v1l, s0, s2, s2c, gat,
    d0w, d0r, d0, d1, dq2, inn_send, inn_recv, oc, gv, gt, gs,
    lsem, ysend, yrecv, ssend, srecv, hsend, hrecv, gsend, grecv, asend, arecv, isend, irecv,
):
    n = lax.axis_index("snode")
    k = lax.axis_index("panel")
    count = lax.axis_size("snode")
    nxt = lax.rem(n + 1, count)
    prv = lax.rem(n + count - 1, count)
    core = lax.rem(n, 2)
    sib = n + 1 - 2 * core
    right, left, opp = lax.rem(k + 1, 4), lax.rem(k + 3, 4), lax.rem(k + 2, 4)
    around = (right, opp, left)

    barrier = pltpu.get_barrier_semaphore()
    for who in ({"panel": left}, {"panel": right}, {"panel": opp}, {"snode": sib}, {"snode": prv}):
        pl.semaphore_signal(barrier, inc=1, device_id=who, device_id_type=MESH)

    def rows(start, size):
        return pl.ds(pl.multiple_of(start, 8), size)

    def local_copy(src, dst, at):
        return pltpu.make_async_copy(src, dst, lsem.at[at])

    def remote(src, dst, ss, rs, who):
        return pltpu.make_async_remote_copy(
            src_ref=src, dst_ref=dst, send_sem=ss, recv_sem=rs, device_id=who, device_id_type=MESH
        )

    loads = [
        local_copy(top, z.at[rows(SHARD * k, SHARD), pl.ds(0, T)], 0),
        local_copy(ufac.at[1, 0], u1, 1),
        local_copy(ufac.at[0, 0], u0, 2),
        local_copy(dinv.at[0, 0], d0w, 3),
        local_copy(ufac.at[2, 0], u2, 4),
        local_copy(dinv.at[1, 0], d1.at[rows(BQ * k, BQ)], 5),
        local_copy(dinv.at[2, 0], dq2, 6),
    ]
    for copy in loads:
        copy.start()
    pl.semaphore_wait(barrier, 5)

    sends = []

    def send(src, dst, ss, rs, who):
        copy = remote(src, dst, ss, rs, who)
        copy.start()
        sends.append(copy)

    def arrived(dst, rs):
        remote(dst, dst, rs, rs, {"panel": right}).wait_recv()

    def piece(shard, c, part):
        return z.at[rows(SHARD * shard + HALF * c + SUB * part, SUB), pl.ds(0, T)]

    def own(part):
        return top.at[rows(HALF * core + SUB * part, SUB), :]

    to_r, to_l = {"panel": right}, {"panel": left}
    send(own(0), piece(k, core, 0), ysend.at[0], yrecv.at[0], to_r)
    send(own(1), piece(k, core, 1), ysend.at[1], yrecv.at[1], to_l)
    send(ufac.at[0, 0], u0r, hsend.at[0], hrecv.at[0], {"snode": nxt})
    send(dinv.at[0, 0], d0r, hsend.at[1], hrecv.at[1], {"snode": nxt})
    send(own(1), piece(k, core, 1), ysend.at[2], yrecv.at[2], to_r)
    send(own(0), piece(k, core, 0), ysend.at[3], yrecv.at[3], to_l)

    def service(at):
        shard, part = ((left, 0), (right, 1), (left, 1), (right, 0), (opp, 0), (opp, 1))[at]
        here = piece(shard, core, part)
        arrived(here, yrecv.at[at])
        if at == 0:
            send(here, here, ysend.at[4], yrecv.at[4], to_r)
        if at == 1:
            send(here, here, ysend.at[5], yrecv.at[5], to_l)
        send(here, here, ssend.at[at], srecv.at[at], {"snode": sib})

    def service_sib(at):
        shard, part = ((left, 0), (right, 1), (left, 1), (right, 0), (opp, 0), (opp, 1))[at]
        arrived(piece(shard, 1 - core, part), srecv.at[at])

    p0 = pm[0, n]
    p1 = pm[1, n]
    lane = lax.broadcasted_iota(jnp.int32, (1, SR), 1)
    h0 = jnp.where(lane < ln[0, p0], rm[pl.ds(p0, 1), :], -1)
    g0 = jnp.where(lane < ln[0, n], rm[pl.ds(n, 1), :], -1)
    r1 = rm[pl.ds(count + n, 1), :]
    g1 = jnp.where(r1 < B, r1 + J0, compose(h0, r1 - B))
    g1 = jnp.where(lane < ln[1, n], g1, -1)
    r2 = rm[pl.ds(2 * count + n, 1), :]
    g2 = jnp.where(lane < ln[2, n], jnp.where(r2 < B, r2 + J1, compose(g1, r2 - B)), -1)
    r2c = rm[pl.ds(2 * count + nxt, 1), :]
    g2c = jnp.where(lane < ln[2, nxt], jnp.where(r2c < B, r2c + J1, compose(g1, r2c - B)), -1)
    lists = jnp.concatenate([g0, g1, g2, g2c, g0, g1, g2, g2c], axis=0)
    gv[...] = jnp.maximum(lists, 0)
    gt[...] = jnp.concatenate([lists.astype(F32)] * 16, axis=0).T
    to_smem = local_copy(gv, gs, 7)
    to_smem.start()

    def scatter(g, vh, vl, tiles):
        @pl.loop(0, tiles)
        def _(i):
            s = one_hot(g, 256 * i, 256)
            here = rows(256 * i, 256)
            vh[here, :] = mm(s, uh[...]).astype(BF16)
            vl[here, :] = mm(s, ul[...]).astype(BF16)

    def load_u(value):
        uh[...], ul[...] = split(value)

    loads[1].wait()
    load_u(u1[...])
    scatter(g1, v1h, v1l, J1 // 256)

    def build(g, s, tiles):
        @pl.loop(0, tiles)
        def _(i):
            s[rows(256 * i, 256), :] = one_hot(g, 256 * i, 256)

    service(0)
    service(1)
    build(g0, s0, T // 256)
    build(g2c, s2c, N2 // 256)
    build(g2, s2, N2 // 256)

    def stream1(shard):
        here = rows(SHARD * shard, SHARD)
        t = z[here, 0:T]
        z[here, J1:N2] = -mm3(t, v1h[0:T, :], v1l[0:T, :])

    def stream0(shard):
        here = rows(SHARD * shard, SHARD)
        t = z[here, 0:T]
        z[here, J0:J1] = -mm3(t, v0h[...], v0l[...])

    loads[0].wait()
    stream1(k)
    service(2)
    service(3)

    for at in (2, 3):
        loads[at].wait()
    arrived(d0r, hrecv.at[1])
    mine0 = p0 == n
    d0_here = rows(BQ * k, BQ)
    d0[d0_here, :] = jnp.where(mine0, d0w[...], d0r[...])

    def gather_d(ref, at):
        for hop in range(3):
            send(ref.at[d0_here], ref.at[d0_here], gsend.at[at, hop], grecv.at[at, hop], {"panel": around[hop]})

    def gathered_d(ref, at):
        for hop in range(3):
            arrived(ref.at[rows(BQ * lax.rem(k + 3 - hop, 4), BQ)], grecv.at[at, hop])

    gather_d(d0, 0)
    loads[5].wait()
    gather_d(d1, 1)

    arrived(u0r, hrecv.at[0])
    load_u(jnp.where(mine0, u0[...], u0r[...]))
    scatter(h0, v0h, v0l, T // 256)
    stream0(k)
    service_sib(0)
    service_sib(1)
    service_sib(2)
    service_sib(3)
    stream1(left)
    stream0(left)
    service(4)
    service(5)
    stream1(right)
    stream0(right)
    service_sib(4)
    service_sib(5)
    stream1(opp)
    stream0(opp)

    to_smem.wait()

    def live(row):
        return gt[rows(RQ * k, RQ), row:row + 1] >= 0.0

    def extract(row, kdim, s):
        @pl.loop(0, RQ, unroll=8)
        def _(a):
            gat[pl.ds(a, 1), 0:kdim] = z[pl.ds(gs[row, RQ * k + a], 1), 0:kdim]

        gh, gl = split(gat[:, 0:kdim])
        inner = mm(gh, s[...]) + mm(gl, s[...])
        return jnp.where(live(row), inner, 0.0)

    def finish_off(level, slot, inner, u):
        uh[...], ul[...] = split(u[...])
        off_out[level, 0] = -mm3(inner, uh[...], ul[...])
        for hop in range(3):
            j = around[hop]
            send(
                off_out.at[level, 0, :, pl.ds(pl.multiple_of(BQ * j, BQ), BQ)],
                oc.at[slot, rows(RQ * k, RQ)],
                asend.at[slot, hop], arecv.at[slot, hop], {"panel": j},
            )
        keep = pltpu.make_async_copy(
            off_out.at[level, 0, :, pl.ds(pl.multiple_of(BQ * k, BQ), BQ)],
            oc.at[slot, rows(RQ * k, RQ)], lsem.at[8 + slot],
        )
        keep.start()
        return keep

    def finish_diag(level, slot, keep, d, u):
        for hop in range(3):
            arrived(oc.at[slot, rows(RQ * lax.rem(k + 3 - hop, 4), RQ)], arecv.at[slot, hop])
        keep.wait()
        diag_out[level, 0] = d - mmf(oc[slot].T, u[...])

    keep0 = finish_off(0, 0, extract(0, T, s0), u0)

    z[J0:J1, 0:T] = z[0:T, J0:J1].T
    gathered_d(d0, 0)
    z[J0:J1, J0:J1] = d0[...] - mm3(z[J0:J1, 0:T], v0h[...], v0l[...])
    z[J0:J1, J1:N2] = -mm3(z[J0:J1, 0:J1], v1h[...], v1l[...])

    @pl.loop(0, 4)
    def _(i):
        here = rows(SHARD * i, SHARD)
        z[here, J1:N2] = z[here, J1:N2] - mm3(z[here, J0:J1], v1h[J0:J1, :], v1l[J0:J1, :])

    z[J1:N2, 0:J1] = z[0:J1, J1:N2].T
    gathered_d(d1, 1)
    z[J1:N2, J1:N2] = d1[...] - mm3(z[J1:N2, 0:J1], v1h[...], v1l[...])

    inn_send[...] = extract(3, N2, s2c)
    send(inn_send, inn_recv, isend.at[0], irecv.at[0], {"snode": nxt})
    inner_mine = extract(2, N2, s2)
    finish_diag(0, 0, keep0, d0w[...], u0)

    @pl.loop(0, RQ, unroll=8)
    def _(a):
        off_out[1, 0, pl.ds(a, 1), :] = z[pl.ds(gs[1, RQ * k + a], 1), J1:N2]

    off_out[1, 0] = jnp.where(live(1), off_out[1, 0], 0.0)
    diag_out[1, 0] = z[rows(J1 + BQ * k, BQ), J1:N2]

    loads[4].wait()
    loads[6].wait()
    arrived(inn_recv, irecv.at[0])
    inner2 = jnp.where(p1 == n, inner_mine, inn_recv[...])
    keep2 = finish_off(2, 1, inner2, u2)
    finish_diag(2, 1, keep2, dq2[...], u2)

    for copy in sends:
        copy.wait_send()


def local(top_inverse, diag_inverse, u_factor, parent_map, lengths, rows_map):
    dma = pltpu.SemaphoreType.DMA
    vm, hbm, sm = (pl.BlockSpec(memory_space=m) for m in (pltpu.VMEM, pl.ANY, pltpu.SMEM))
    return pl.pallas_call(
        kernel,
        out_shape=(
            jax.ShapeDtypeStruct((3, 1, BQ, B), F32),
            jax.ShapeDtypeStruct((3, 1, RQ, B), F32),
        ),
        in_specs=[hbm, hbm, hbm, sm, sm, vm],
        out_specs=(vm, vm),
        scratch_shapes=[
            pltpu.VMEM((N2, N2), F32),
            pltpu.VMEM((SR, B), F32),
            pltpu.VMEM((SR, B), F32),
            pltpu.VMEM((SR, B), F32),
            pltpu.VMEM((SR, B), F32),
            pltpu.VMEM((SR, B), BF16),
            pltpu.VMEM((SR, B), BF16),
            pltpu.VMEM((T, B), BF16),
            pltpu.VMEM((T, B), BF16),
            pltpu.VMEM((J1, B), BF16),
            pltpu.VMEM((J1, B), BF16),
            pltpu.VMEM((T, SR), BF16),
            pltpu.VMEM((N2, SR), BF16),
            pltpu.VMEM((N2, SR), BF16),
            pltpu.VMEM((RQ, N2), F32),
            pltpu.VMEM((BQ, B), F32),
            pltpu.VMEM((BQ, B), F32),
            pltpu.VMEM((B, B), F32),
            pltpu.VMEM((B, B), F32),
            pltpu.VMEM((BQ, B), F32),
            pltpu.VMEM((RQ, SR), F32),
            pltpu.VMEM((RQ, SR), F32),
            pltpu.VMEM((2, SR, BQ), F32),
            pltpu.VMEM((8, SR), jnp.int32),
            pltpu.VMEM((SR, 128), F32),
            pltpu.SMEM((8, SR), jnp.int32),
            dma((10,)), dma((6,)), dma((6,)), dma((6,)), dma((6,)),
            dma((2,)), dma((2,)), dma((2, 3)), dma((2, 3)), dma((2, 3)), dma((2, 3)),
            dma((1,)), dma((1,)),
        ],
        compiler_params=pltpu.CompilerParams(
            collective_id=0, has_side_effects=True, vmem_limit_bytes=62 * 1024 * 1024
        ),
    )(
        top_inverse, diag_inverse, u_factor, parent_map, lengths,
        rows_map.reshape(3 * rows_map.shape[1], SR),
    )


def solution(mesh):
    return jax.shard_map(
        local,
        mesh=mesh,
        in_specs=(
            P("panel", None),
            P(None, "snode", "panel", None),
            P(None, "snode", None, None),
            P(),
            P(),
            P(),
        ),
        out_specs=(P(None, "snode", "panel", None), P(None, "snode", "panel", None)),
        check_vma=False,
    )
```
